128 devices in a mesh: clu: 8 (over z, core), row: 16 (over y, x).
Axes of the slice: x: 4, y: 4, z: 4, core: 2. Of those that a mesh axis runs over, the one named last changes fastest.
Arguments:
- rhs: float32 [256, 524288], P(None, ('clu', 'row')), may hold values from -6 to 6
- linv: float32 [2048, 256, 256], P(('clu', 'row'))
- w_one: float32 [524288, 128], P(('clu', 'row')), may hold values from -1.5 to 1.5
- w_two: float32 [524288, 128], P(('clu', 'row')), may hold values from -1.5 to 1.5
- held: int32 [16], replicated, may hold values from 0 to 15, each once
- ranks: int32 [12], replicated, may hold values from 16 to 128, as said below
Outputs:
- solved: float32 [256, 524288], P(None, ('clu', 'row'))
The draws below stay inside these ranges and needn't reach their ends.
Inputs may be any that keep to these rules, and one draw needn't show every extreme that they name: `ranks`: entries 0 to 7 are the level-one blocks of subtrees in order (two a subtree), the rest the level-two blocks; some entry equals 128. `held`: a permutation of the clusters.
All inputs are finite; a program needn't handle non-finite values.
Results may differ from the reference program's by a relative error of at most 0.0001.
Values sent between devices are 32-bit elements; how exact they have to be, the bound alone decides.
No kernel may reach another device: no remote copies, remote signals or barrier semaphores. Data moves between devices by JAX's collectives and lax.ppermute only.
A program may use at most 128 MiB of HBM per device.

```python
import math
import jax
import jax.numpy as jnp
from jax import lax

RANK = 128
LEAF = 256
CLUSTERS = 16
CLUSTER_ROWS = 32768
ORDER = 524288
COLS = 256


def draw_linv(key, part):
    key_diag, key_low = jax.random.split(jax.random.fold_in(key, 11))
    blocks = ORDER // LEAF
    diagonal = jax.random.uniform(key_diag, (blocks, LEAF), jnp.float32, 0.8, 1.6)
    lower = jax.random.normal(key_low, (blocks, LEAF, LEAF), jnp.float32) * (0.6 / LEAF ** 0.5)
    row_ids = jnp.arange(LEAF)[:, None]
    col_ids = jnp.arange(LEAF)[None, :]
    strict = (row_ids > col_ids).astype(jnp.float32)
    ident = (row_ids == col_ids).astype(jnp.float32)
    return lower * strict[None] + diagonal[:, :, None] * ident[None]


def draw_ranks(key, part):
    key_vals, key_spot = jax.random.split(jax.random.fold_in(key, 23))
    count = CLUSTERS * 3 // 4
    values = jax.random.randint(key_vals, (count,), max(1, RANK // 8), RANK + 1, jnp.int32)
    spot = jax.random.randint(key_spot, (), 0, count, jnp.int32)
    return jnp.where(jnp.arange(count) == spot, RANK, values).astype(jnp.int32)


def shard_levels(rng, shape, shards, low, largest):
    level = 1.0
    for dim, shards_of in shards:
        steps = jax.random.uniform(jax.random.fold_in(jax.random.fold_in(rng, 6), dim), (shards_of,), jnp.float32, low / len(shards), largest / len(shards))
        level = level * jnp.repeat(jnp.exp(steps), shape[dim] // shards_of).reshape((-1,) + (1,) * (len(shape) - 1 - dim))
    return level


def gaussian(rng, extent, width, limit, shards=(), kind=jnp.bfloat16):
    values = jax.random.normal(rng, extent, jnp.float32) * width
    if len(shards) > 0:
        values = shard_levels(rng, extent, shards, -0.22, 0.18) * values
    return jnp.clip(values, min=-limit, max=limit).astype(kind)


def setup_inputs(seed: int = 0) -> dict:
    keys = jax.random.split(jax.random.key(seed), 7)
    return {
        "rhs": gaussian(keys[0], (COLS, ORDER), 1.0, 6.0, ((1, 128),), jnp.float32),
        "linv": draw_linv(jax.random.fold_in(keys[6], 71), 0),
        "w_one": gaussian(keys[2], (ORDER, RANK), 0.25, 1.5, ((0, 128),), jnp.float32),
        "w_two": gaussian(keys[3], (ORDER, RANK), 0.25, 1.5, ((0, 128),), jnp.float32),
        "held": jax.random.permutation(keys[4], CLUSTERS).astype(jnp.int32),
        "ranks": draw_ranks(jax.random.fold_in(keys[6], 71), 0),
    }


def leaf_apply(values, inverse):
    blocks = inverse.shape[0]
    leaf_width = inverse.shape[1]
    pieces = values.reshape(values.shape[0], blocks, leaf_width).transpose(1, 0, 2)
    result = jnp.einsum('bcj,bij->bci', pieces, inverse, precision=lax.Precision.HIGHEST)
    return result.transpose(1, 0, 2).reshape(values.shape[0], blocks * leaf_width)

def rank_mask(ranks, block_index):
    return (jnp.arange(RANK) < ranks[block_index]).astype(jnp.float32)

def reference(rhs, linv, w_one, w_two, held, ranks):
    cluster_rows = CLUSTER_ROWS
    scaling = 1.0 / math.sqrt(cluster_rows)
    source = rhs.reshape(COLS, CLUSTERS, cluster_rows).transpose(1, 0, 2)
    inverse = linv.reshape(CLUSTERS, cluster_rows // LEAF, LEAF, LEAF)
    first_weights = w_one.reshape(CLUSTERS, cluster_rows, RANK)
    second_weights = w_two.reshape(CLUSTERS, cluster_rows, RANK)
    solved = jax.vmap(leaf_apply)(source, inverse)
    slot_ids = jnp.arange(CLUSTERS, dtype=jnp.int32)
    where_is = lax.optimization_barrier(jnp.sum(jnp.where(held[None, :] == slot_ids[:, None], slot_ids[None, :], 0), axis=1)).astype(jnp.int32)
    highest = lax.Precision.HIGHEST
    for subtree in range(CLUSTERS // 4):
        group_zero = where_is[4 * subtree]
        group_one = where_is[4 * subtree + 1]
        group_two = where_is[4 * subtree + 2]
        group_three = where_is[4 * subtree + 3]
        coef_one = jnp.dot(solved[group_zero], first_weights[group_zero], precision=highest) * scaling
        coef_one = coef_one * rank_mask(ranks, 2 * subtree)[None, :]
        current = source[group_one] - jnp.dot(coef_one, first_weights[group_one].T, precision=highest)
        solved = solved.at[group_one].set(leaf_apply(current, inverse[group_one]))
        coef_two = jnp.dot(solved[group_zero], second_weights[group_zero], precision=highest) * scaling
        coef_two = coef_two + jnp.dot(solved[group_one], second_weights[group_one], precision=highest) * scaling
        coef_two = coef_two * rank_mask(ranks, CLUSTERS // 2 + subtree)[None, :]
        current = source[group_two] - jnp.dot(coef_two, second_weights[group_two].T, precision=highest)
        solved = solved.at[group_two].set(leaf_apply(current, inverse[group_two]))
        later = source[group_three] - jnp.dot(coef_two, second_weights[group_three].T, precision=highest)
        coef_three = jnp.dot(solved[group_two], first_weights[group_two], precision=highest) * scaling
        coef_three = coef_three * rank_mask(ranks, 2 * subtree + 1)[None, :]
        later = later - jnp.dot(coef_three, first_weights[group_three].T, precision=highest)
        solved = solved.at[group_three].set(leaf_apply(later, inverse[group_three]))
    return solved.transpose(1, 0, 2).reshape(COLS, ORDER)
```

```python
import functools
import math

import jax
import jax.numpy as jnp
from jax import lax
from jax.experimental import pallas as pl
from jax.experimental.pallas import tpu as pltpu
from jax.sharding import Mesh, PartitionSpec as P


AXES = ("z", "core", "yh", "yl", "x")
SLOT = ("z", "core", "yh")
LOCAL = ("yl", "x")
LEAVES_PER_STEP = 4


def halves(value):
    high = value.astype(jnp.bfloat16)
    low = (value - high.astype(jnp.float32)).astype(jnp.bfloat16)
    return high, low


def main_kernel(held, rhs, linv, w_one, w_two, z_out, high_out, low_out, msg, total):
    step = pl.program_id(0)
    cols = rhs.shape[0]
    leaf = linv.shape[1]
    rank = w_one.shape[1]

    @pl.when(step == 0)
    def _():
        total[...] = jnp.zeros_like(total)

    for j in range(linv.shape[0]):
        span = slice(j * leaf, (j + 1) * leaf)
        a = w_one[span, :]
        e = w_two[span, :]
        x = jnp.concatenate([rhs[:, span], a.T, e.T], axis=0)
        x_high, x_low = halves(x)
        l_high, l_low = halves(linv[j])
        y = lax.dot_general(
            jnp.concatenate([x_high, x_high, x_low], axis=1),
            jnp.concatenate([l_high, l_low, l_high], axis=1),
            (((1,), (1,)), ((), ())),
            preferred_element_type=jnp.float32,
        )
        y_high, y_low = halves(y)
        z_out[:, span] = y[:cols]
        high_out[:, span] = y_high[cols:]
        low_out[:, span] = y_low[cols:]
        w_high, w_low = halves(jnp.concatenate([a, e], axis=1))
        total[...] += jnp.dot(
            jnp.concatenate([y_high, y_high, y_low], axis=1),
            jnp.concatenate([w_high, w_low, w_high], axis=0),
            preferred_element_type=jnp.float32,
        )

    @pl.when(step == pl.num_programs(0) - 1)
    def _():
        slot = (lax.axis_index("z") * 2 + lax.axis_index("core")) * 2 + lax.axis_index("yh")
        position = lax.rem(held[slot], 4)
        parts = msg.shape[0]
        wide = cols // parts
        narrow = rank // parts
        for i in range(parts):
            rows = slice(i * wide, (i + 1) * wide)
            msg[i, :wide, :] = total[rows, :rank]
            msg[i, wide:, :] = total[rows, rank:]

        @pl.when(position == 1)
        def _():
            for i in range(parts):
                rows = slice(cols + i * narrow, cols + (i + 1) * narrow)
                msg[i, :narrow, :] = total[rows, rank:]

        @pl.when(position == 2)
        def _():
            for i in range(parts):
                rows = slice(cols + rank + i * narrow, cols + rank + (i + 1) * narrow)
                msg[i, wide : wide + narrow, :] = total[rows, :rank]


def main_call(rhs, linv, w_one, w_two, held, parts):
    cols, rows = rhs.shape
    leaf = linv.shape[1]
    rank = w_one.shape[1]
    per = LEAVES_PER_STEP
    return pl.pallas_call(
        main_kernel,
        grid_spec=pltpu.PrefetchScalarGridSpec(
            num_scalar_prefetch=1,
            grid=(rows // (leaf * per),),
            in_specs=[
                pl.BlockSpec((cols, leaf * per), lambda i, h: (0, i)),
                pl.BlockSpec((per, leaf, leaf), lambda i, h: (i, 0, 0)),
                pl.BlockSpec((leaf * per, rank), lambda i, h: (i, 0)),
                pl.BlockSpec((leaf * per, rank), lambda i, h: (i, 0)),
            ],
            out_specs=[
                pl.BlockSpec((cols, leaf * per), lambda i, h: (0, i)),
                pl.BlockSpec((2 * rank, leaf * per), lambda i, h: (0, i)),
                pl.BlockSpec((2 * rank, leaf * per), lambda i, h: (0, i)),
                pl.BlockSpec((parts, 2 * cols // parts, rank), lambda i, h: (0, 0, 0)),
            ],
            scratch_shapes=[pltpu.VMEM((cols + 2 * rank, 2 * rank), jnp.float32)],
        ),
        out_shape=[
            jax.ShapeDtypeStruct((cols, rows), jnp.float32),
            jax.ShapeDtypeStruct((2 * rank, rows), jnp.bfloat16),
            jax.ShapeDtypeStruct((2 * rank, rows), jnp.bfloat16),
            jax.ShapeDtypeStruct((parts, 2 * cols // parts, rank), jnp.float32),
        ],
        compiler_params=pltpu.CompilerParams(vmem_limit_bytes=60 * 2**20),
        name="leaves",
    )(held, rhs, linv, w_one, w_two)


def pick_kernel(held, got, out):
    slots = got.shape[0]
    wide = got.shape[1] // 2
    rank = got.shape[2]
    slot = (lax.axis_index("z") * 2 + lax.axis_index("core")) * 2 + lax.axis_index("yh")
    base = (held[slot] // 4) * 4
    place = [jnp.int32(0)] * 3
    for s in range(slots):
        for p in range(3):
            place[p] = jnp.where(held[s] == base + p, s, place[p])
    block_a = got[place[0]]
    block_b = got[place[1]]
    block_c = got[place[2]]
    narrow = (out.shape[1] - 3 * wide) // 2
    pieces = jnp.concatenate(
        [
            block_a[:wide],
            block_a[wide:] + block_b[wide:],
            block_c[:wide],
            block_b[:narrow],
            block_c[wide : wide + narrow],
        ],
        axis=0,
    )
    for i in range(out.shape[0]):
        out[i] = pieces


def pick_call(got, held, parts):
    slots, height, rank = got.shape
    out_height = 3 * height // 2 + 2 * (rank // parts)
    return pl.pallas_call(
        pick_kernel,
        in_specs=[
            pl.BlockSpec(memory_space=pltpu.SMEM),
            pl.BlockSpec(memory_space=pltpu.VMEM),
        ],
        out_specs=pl.BlockSpec(memory_space=pltpu.VMEM),
        out_shape=jax.ShapeDtypeStruct((parts, out_height, rank), jnp.float32),
        name="pick",
    )(held, got)


def last_kernel(scaling, held, ranks, got, z, high, low, out, c_left):
    cols = z.shape[0]
    parts, height, rank = got.shape
    wide = cols // parts
    narrow = rank // parts
    slot = (lax.axis_index("z") * 2 + lax.axis_index("core")) * 2 + lax.axis_index("yh")
    cluster = held[slot]
    position = lax.rem(cluster, 4)
    tree = cluster // 4

    @pl.when(pl.program_id(0) == 0)
    def _():
        def mat(start, size):
            return got[:, start : start + size, :].reshape(parts * size, rank)

        def masked(value, limit):
            lane = lax.broadcasted_iota(jnp.int32, value.shape, 1)
            return jnp.where(lane < limit, value * scaling, 0.0)

        def times(left, right):
            return jnp.dot(
                left, right, precision=lax.Precision.HIGHEST, preferred_element_type=jnp.float32
            )

        one = masked(mat(0, wide), ranks[2 * tree])
        two = mat(wide, wide) - times(one, mat(3 * wide, narrow))
        two = masked(two, ranks[8 + tree])
        three = mat(2 * wide, wide) - times(two, mat(3 * wide + narrow, narrow))
        three = masked(three, ranks[2 * tree + 1])
        left = jnp.where(position == 1, one, jnp.where(position == 3, three, 0.0))
        right = jnp.where(position >= 2, two, 0.0)
        c_high, c_low = halves(jnp.concatenate([left, right], axis=1))
        c_left[...] = jnp.concatenate([c_high, c_high, c_low], axis=1)

    out[...] = z[...] - jnp.dot(
        c_left[...],
        jnp.concatenate([high[...], low[...], high[...]], axis=0),
        preferred_element_type=jnp.float32,
    )


def last_call(got, z, high, low, held, ranks, scaling):
    cols, rows = z.shape
    rank2 = high.shape[0]
    block = 1024
    return pl.pallas_call(
        functools.partial(last_kernel, scaling),
        grid_spec=pltpu.PrefetchScalarGridSpec(
            num_scalar_prefetch=2,
            grid=(rows // block,),
            in_specs=[
                pl.BlockSpec(got.shape, lambda i, h, r: (0, 0, 0)),
                pl.BlockSpec((cols, block), lambda i, h, r: (0, i)),
                pl.BlockSpec((rank2, block), lambda i, h, r: (0, i)),
                pl.BlockSpec((rank2, block), lambda i, h, r: (0, i)),
            ],
            out_specs=pl.BlockSpec((cols, block), lambda i, h, r: (0, i)),
            scratch_shapes=[pltpu.VMEM((cols, 3 * rank2), jnp.bfloat16)],
        ),
        out_shape=jax.ShapeDtypeStruct((cols, rows), jnp.float32),
        compiler_params=pltpu.CompilerParams(vmem_limit_bytes=60 * 2**20),
        name="correct",
    )(held, ranks, got, z, high, low)


def swap(value, axes):
    return lax.all_to_all(value, axes, 0, 0, tiled=True)


def shards(scaling, rhs, linv, w_one, w_two, held, ranks):
    parts = lax.axis_size(LOCAL)
    slots = lax.axis_size(SLOT)
    z, high, low, msg = main_call(rhs, linv, w_one, w_two, held, parts)
    own = jnp.sum(swap(msg, LOCAL), axis=0)
    got = swap(jnp.broadcast_to(own[None], (slots,) + own.shape), SLOT)
    shared = swap(pick_call(got, held, parts), LOCAL)
    return last_call(shared, z, high, low, held, ranks, scaling)


def solution(mesh):
    fine = Mesh(mesh.devices.reshape(4, 2, 2, 2, 4), AXES)
    scaling = 1.0 / math.sqrt(32768)
    in_specs = (P(None, AXES), P(AXES, None, None), P(AXES, None), P(AXES, None), P(), P())
    return jax.shard_map(
        functools.partial(shards, scaling),
        mesh=fine,
        in_specs=in_specs,
        out_specs=P(None, AXES),
        check_vma=False,
    )
```

```python
import functools
import math

import jax
import jax.numpy as jnp
from jax import lax
from jax.experimental import pallas as pl
from jax.experimental.pallas import tpu as pltpu
from jax.sharding import Mesh, PartitionSpec as P


AXES = ("z", "core", "yh", "yl", "x")
SLOT = ("z", "yh")
LOCAL = ("yl", "x")
GROUP = 2
CHUNK = 512


def halves(value):
    high = value.astype(jnp.bfloat16)
    low = (value - high.astype(jnp.float32)).astype(jnp.bfloat16)
    return high, low


def split3(value):
    high, low = halves(value)
    return jnp.concatenate([high, high, low], axis=1)


def nt(left, right):
    return lax.dot_general(
        left, right, (((1,), (1,)), ((), ())), preferred_element_type=jnp.float32
    )


def own_slot():
    return (lax.axis_index("z") * 2 + lax.axis_index("core")) * 2 + lax.axis_index("yh")


def main_kernel(
    held_in, rhs, linv, w_one, w_two, z, high, low, msg,
    held, rhs_v, linv_v, w_v, total, even, odd, held_sem, sems,
):
    cols = rhs.shape[0]
    leaves, leaf, _ = linv.shape
    rank = w_one.shape[1]
    groups = leaves // GROUP
    parts = msg.shape[0]
    wide = cols // parts
    narrow = rank // parts

    def copies(g):
        rows = pl.ds(g * (GROUP * leaf), GROUP * leaf)
        pair = pl.ds(g * GROUP, GROUP)
        return [
            pltpu.make_async_copy(rhs.at[:, rows], rhs_v.at[:, rows], sems.at[0, g]),
            pltpu.make_async_copy(linv.at[pair], linv_v.at[pair], sems.at[1, g]),
            pltpu.make_async_copy(w_one.at[rows], w_v.at[0, rows], sems.at[2, g]),
            pltpu.make_async_copy(w_two.at[rows], w_v.at[1, rows], sems.at[3, g]),
        ]

    held_copy = pltpu.make_async_copy(held_in, held, held_sem)
    held_copy.start()
    for g in range(groups):
        for copy in copies(g):
            copy.start()
    msg[...] = jnp.zeros_like(msg)
    held_copy.wait()
    position = lax.rem(held[own_slot()], 4)

    def span_of(i):
        return pl.ds(pl.multiple_of(i * leaf, leaf), leaf)

    def wait(g):
        for copy in copies(g):
            copy.wait()

    def each_leaf(solve, couple):
        wait(0)
        solve(0, even)

        def pair(k, carry):
            wait(k + 1)
            couple(2 * k, even)
            solve(2 * k + 1, odd)
            couple(2 * k + 1, odd)
            solve(2 * k + 2, even)
            return carry

        lax.fori_loop(0, groups - 1, pair, 0)
        couple(leaves - 2, even)
        solve(leaves - 1, odd)
        couple(leaves - 1, odd)

    def leaf_product(x, i):
        l_high, l_low = halves(linv_v[i])
        return nt(split3(x), jnp.concatenate([l_high, l_low, l_high], axis=1))

    @pl.when(position == 0)
    def _():
        total[:cols] = jnp.zeros((cols, 2 * rank), jnp.float32)

        def solve(i, kept):
            span = span_of(i)
            y = leaf_product(rhs_v[:, span], i)
            z[:, span] = y
            y_high, y_low = halves(y)
            kept[0, :cols] = y_high
            kept[1, :cols] = y_low

        def couple(i, kept):
            span = span_of(i)
            w = jnp.concatenate([w_v[0, span, :], w_v[1, span, :]], axis=1)
            w_high, w_low = halves(w)
            y_high = kept[0, :cols]
            total[:cols] += jnp.dot(
                jnp.concatenate([y_high, y_high, kept[1, :cols]], axis=1),
                jnp.concatenate([w_high, w_low, w_high], axis=0),
                preferred_element_type=jnp.float32,
            )

        each_leaf(solve, couple)
        for i in range(parts):
            rows = slice(i * wide, (i + 1) * wide)
            msg[i, :wide, :] = total[rows, :rank]
            msg[i, wide:, :] = total[rows, rank:]

    @pl.when((position == 1) | (position == 2))
    def _():
        mine = position - 1
        other = 2 - position
        total[...] = jnp.zeros_like(total)

        def solve(i, kept):
            span = span_of(i)
            x = jnp.concatenate([rhs_v[:, span], w_v[mine, span, :].T], axis=0)
            y = leaf_product(x, i)
            y_high, y_low = halves(y)
            z[:, span] = y[:cols]
            high[:rank, span] = y_high[cols:]
            low[:rank, span] = y_low[cols:]
            kept[0] = y_high
            kept[1] = y_low

        def couple(i, kept):
            w_high, w_low = halves(w_v[other, span_of(i), :])
            right = jnp.concatenate([w_high, w_low], axis=1)
            total[...] += jnp.dot(
                jnp.concatenate([kept[0], kept[1]], axis=1),
                jnp.concatenate([right, right], axis=0),
                preferred_element_type=jnp.float32,
            )

        each_leaf(solve, couple)
        total[:, :rank] = total[:, :rank] + total[:, rank:]
        for i in range(parts):
            rows = slice(i * wide, (i + 1) * wide)
            cross = slice(cols + i * narrow, cols + (i + 1) * narrow)

            @pl.when(position == 1)
            def _():
                msg[i, :narrow, :] = total[cross, :rank]
                msg[i, wide:, :] = total[rows, :rank]

            @pl.when(position == 2)
            def _():
                msg[i, :wide, :] = total[rows, :rank]
                msg[i, wide : wide + narrow, :] = total[cross, :rank]

    @pl.when(position == 3)
    def _():
        def solve(i, kept):
            span = span_of(i)
            x = jnp.concatenate(
                [rhs_v[:, span], w_v[0, span, :].T, w_v[1, span, :].T], axis=0
            )
            y = leaf_product(x, i)
            y_high, y_low = halves(y[cols:])
            z[:, span] = y[:cols]
            high[:, span] = y_high
            low[:, span] = y_low

        each_leaf(solve, lambda i, kept: None)


def main_call(rhs, linv, w_one, w_two, held, parts):
    cols, rows = rhs.shape
    leaves, leaf, _ = linv.shape
    rank = w_one.shape[1]
    arrays = [
        pltpu.with_memory_space_constraint(v, pltpu.HBM)
        for v in (held, rhs, linv, w_one, w_two)
    ]
    return pl.pallas_call(
        main_kernel,
        in_specs=[pl.BlockSpec(memory_space=pltpu.HBM)] * 5,
        out_specs=[pl.BlockSpec(memory_space=pltpu.VMEM)] * 4,
        out_shape=[
            pltpu.VMEM((cols, rows), jnp.float32),
            pltpu.VMEM((2 * rank, rows), jnp.bfloat16),
            pltpu.VMEM((2 * rank, rows), jnp.bfloat16),
            pltpu.VMEM((parts, 2 * cols // parts, rank), jnp.float32),
        ],
        scratch_shapes=[
            pltpu.SMEM(held.shape, jnp.int32),
            pltpu.VMEM((cols, rows), jnp.float32),
            pltpu.VMEM((leaves, leaf, leaf), jnp.float32),
            pltpu.VMEM((2, rows, rank), jnp.float32),
            pltpu.VMEM((cols + rank, 2 * rank), jnp.float32),
            pltpu.VMEM((2, cols + rank, leaf), jnp.bfloat16),
            pltpu.VMEM((2, cols + rank, leaf), jnp.bfloat16),
            pltpu.SemaphoreType.DMA(()),
            pltpu.SemaphoreType.DMA((4, leaves // GROUP)),
        ],
        compiler_params=pltpu.CompilerParams(vmem_limit_bytes=40 * 2**20),
        name="leaves",
    )(*arrays)


def fold_kernel(got, out):
    value = got[0]
    for i in range(1, got.shape[0]):
        value = value + got[i]
    for i in range(out.shape[0]):
        out[i] = value


def fold_call(got, count):
    return pl.pallas_call(
        fold_kernel,
        in_specs=[pl.BlockSpec(memory_space=pltpu.VMEM)],
        out_specs=pl.BlockSpec(memory_space=pltpu.VMEM),
        out_shape=pltpu.VMEM((count,) + got.shape[1:], jnp.float32),
        compiler_params=pltpu.CompilerParams(vmem_limit_bytes=4 * 2**20),
        name="fold",
    )(pltpu.with_memory_space_constraint(got, pltpu.VMEM))


def pick_kernel(held, got, own, other):
    height, rank = own.shape
    wide = got.shape[1] // 2
    narrow = (height - 3 * wide) // 2
    core = lax.axis_index("core")
    for out, where in ((own, core), (other, 1 - core)):
        slot = (lax.axis_index("z") * 2 + where) * 2 + lax.axis_index("yh")
        base = (held[slot] // 4) * 4
        blocks = []
        for p in range(3):
            place = jnp.int32(0)
            here = jnp.int32(0)
            for s in range(2 * got.shape[0]):
                hit = held[s] == base + p
                place = jnp.where(hit, (s // 4) * 2 + s % 2, place)
                here = jnp.where(hit & (core == (s // 2) % 2), 1, here)
            blocks.append(jnp.where(here == 1, got[place], 0.0))
        a, b, c = blocks
        out[:wide] = a[:wide]
        out[wide : 2 * wide] = a[wide:] + b[wide:]
        out[2 * wide : 3 * wide] = c[:wide]
        out[3 * wide : 3 * wide + narrow] = b[:narrow]
        out[3 * wide + narrow :] = c[wide : wide + narrow]


def pick_call(got, held, parts):
    slots, height, rank = got.shape
    out_height = 3 * height // 2 + 2 * (rank // parts)
    return pl.pallas_call(
        pick_kernel,
        in_specs=[
            pl.BlockSpec(memory_space=pltpu.SMEM),
            pl.BlockSpec(memory_space=pltpu.VMEM),
        ],
        out_specs=[pl.BlockSpec(memory_space=pltpu.VMEM)] * 2,
        out_shape=[pltpu.VMEM((out_height, rank), jnp.float32)] * 2,
        compiler_params=pltpu.CompilerParams(vmem_limit_bytes=4 * 2**20),
        name="pick",
    )(held, pltpu.with_memory_space_constraint(got, pltpu.VMEM))


def last_kernel(scaling, held, ranks, got, z, high, low, out, solved, sems):
    cols, rows = z.shape
    parts, height, rank = got.shape
    wide = cols // parts
    narrow = rank // parts
    cluster = held[own_slot()]
    position = lax.rem(cluster, 4)
    tree = cluster // 4
    count = rows // CHUNK

    def mat(start, size):
        return got[:, start : start + size, :].reshape(parts * size, rank)

    def masked(value, limit):
        lane = lax.broadcasted_iota(jnp.int32, value.shape, 1)
        return jnp.where(lane < limit, value * scaling, 0.0)

    def times(left, right):
        return jnp.dot(
            left, right, precision=lax.Precision.HIGHEST, preferred_element_type=jnp.float32
        )

    def first():
        return masked(mat(0, wide), ranks[2 * tree])

    def second():
        value = mat(wide, wide) - times(first(), mat(3 * wide, narrow))
        return masked(value, ranks[8 + tree])

    def send(source, i):
        span = pl.ds(i * CHUNK, CHUNK)
        return pltpu.make_async_copy(source.at[:, span], out.at[:, span], sems.at[i])

    def correct(coef):
        depth = coef.shape[1]
        left = split3(coef)
        for i in range(count):
            span = slice(i * CHUNK, (i + 1) * CHUNK)
            h = high[:depth, span]
            solved[:, span] = z[:, span] - jnp.dot(
                left,
                jnp.concatenate([h, low[:depth, span], h], axis=0),
                preferred_element_type=jnp.float32,
            )
            send(solved, i).start()
        for i in range(count):
            send(solved, i).wait()

    @pl.when(position == 0)
    def _():
        for i in range(count):
            send(z, i).start()
        for i in range(count):
            send(z, i).wait()

    @pl.when(position == 1)
    def _():
        correct(first())

    @pl.when(position == 2)
    def _():
        correct(second())

    @pl.when(position == 3)
    def _():
        two = second()
        value = mat(2 * wide, wide) - times(two, mat(3 * wide + narrow, narrow))
        correct(jnp.concatenate([masked(value, ranks[2 * tree + 1]), two], axis=1))


def last_call(got, z, high, low, held, ranks, scaling):
    cols, rows = z.shape
    arrays = [pltpu.with_memory_space_constraint(v, pltpu.VMEM) for v in (got, z, high, low)]
    return pl.pallas_call(
        functools.partial(last_kernel, scaling),
        in_specs=[pl.BlockSpec(memory_space=pltpu.SMEM)] * 2
        + [pl.BlockSpec(memory_space=pltpu.VMEM)] * 4,
        out_specs=pl.BlockSpec(memory_space=pltpu.HBM),
        out_shape=pltpu.HBM((cols, rows), jnp.float32),
        scratch_shapes=[
            pltpu.VMEM((cols, rows), jnp.float32),
            pltpu.SemaphoreType.DMA((rows // CHUNK,)),
        ],
        compiler_params=pltpu.CompilerParams(vmem_limit_bytes=16 * 2**20),
        name="correct",
    )(held, ranks, *arrays)


def swap(value, axes):
    return lax.all_to_all(value, axes, 0, 0, tiled=True)


def copied(value, count):
    return jnp.broadcast_to(value[None], (count,) + value.shape)


def shards(scaling, rhs, linv, w_one, w_two, held, ranks):
    parts = lax.axis_size(LOCAL)
    z, high, low, msg = main_call(rhs, linv, w_one, w_two, held, parts)
    got = swap(fold_call(swap(msg, LOCAL), lax.axis_size(SLOT)), SLOT)
    mine, other = pick_call(got, held, parts)
    mine = mine + lax.ppermute(other, "core", [(0, 1), (1, 0)])
    shared = swap(copied(mine, parts), LOCAL)
    return last_call(shared, z, high, low, held, ranks, scaling)


def solution(mesh):
    fine = Mesh(mesh.devices.reshape(4, 2, 2, 2, 4), AXES)
    scaling = 1.0 / math.sqrt(32768)
    in_specs = (P(None, AXES), P(AXES, None, None), P(AXES, None), P(AXES, None), P(), P())
    return jax.shard_map(
        functools.partial(shards, scaling),
        mesh=fine,
        in_specs=in_specs,
        out_specs=P(None, AXES),
        check_vma=False,
    )
```

```python
import functools
import math

import jax
import jax.numpy as jnp
from jax import lax
from jax.experimental import pallas as pl
from jax.experimental.pallas import tpu as pltpu
from jax.sharding import PartitionSpec as P


AXES = ("clu", "row")
GROUP = 2
CHUNK = 512
PER_BLOCK = 8
TILE = 8


def halves(value):
    high = value.astype(jnp.bfloat16)
    low = (value - high.astype(jnp.float32)).astype(jnp.bfloat16)
    return high, low


def split3(value):
    high, low = halves(value)
    return jnp.concatenate([high, high, low], axis=1)


def nt(left, right):
    return lax.dot_general(
        left, right, (((1,), (1,)), ((), ())), preferred_element_type=jnp.float32
    )


def own_slot():
    device = lax.axis_index("clu") * lax.axis_size("row") + lax.axis_index("row")
    return device // PER_BLOCK


def main_kernel(
    held_in, rhs, linv, w_one, w_two, z, lw, msg,
    held, rhs_v, linv_v, w_v, total, even, odd, held_sem, sems,
):
    cols = rhs.shape[0]
    leaves, leaf, _ = linv.shape
    rank = w_one.shape[1]
    groups = leaves // GROUP
    half = cols // 2

    def put(j, block):
        msg[pl.ds(j, half, stride=4), :] = block

    def copies(g):
        rows = pl.ds(g * (GROUP * leaf), GROUP * leaf)
        pair = pl.ds(g * GROUP, GROUP)
        return [
            pltpu.make_async_copy(rhs.at[:, rows], rhs_v.at[:, rows], sems.at[0, g]),
            pltpu.make_async_copy(linv.at[pair], linv_v.at[pair], sems.at[1, g]),
            pltpu.make_async_copy(w_one.at[rows], w_v.at[0, rows], sems.at[2, g]),
            pltpu.make_async_copy(w_two.at[rows], w_v.at[1, rows], sems.at[3, g]),
        ]

    held_copy = pltpu.make_async_copy(held_in, held, held_sem)
    held_copy.start()
    for g in range(groups):
        for copy in copies(g):
            copy.start()
    msg[...] = jnp.zeros_like(msg)
    held_copy.wait()
    position = lax.rem(held[own_slot()], 4)

    def span_of(i):
        return pl.ds(pl.multiple_of(i * leaf, leaf), leaf)

    def wait(g):
        for copy in copies(g):
            copy.wait()

    def each_leaf(solve, couple):
        wait(0)
        solve(0, even)

        def pair(k, carry):
            wait(k + 1)
            couple(2 * k, even)
            solve(2 * k + 1, odd)
            couple(2 * k + 1, odd)
            solve(2 * k + 2, even)
            return carry

        lax.fori_loop(0, groups - 1, pair, 0)
        couple(leaves - 2, even)
        solve(leaves - 1, odd)
        couple(leaves - 1, odd)

    def leaf_product(x, i):
        l_high, l_low = halves(linv_v[i])
        return nt(split3(x), jnp.concatenate([l_high, l_low, l_high], axis=1))

    @pl.when(position == 0)
    def _():
        total[:cols] = jnp.zeros((cols, 2 * rank), jnp.float32)

        def solve(i, kept):
            span = span_of(i)
            y = leaf_product(rhs_v[:, span], i)
            z[:, span] = y
            kept[:cols] = y

        def couple(i, kept):
            span = span_of(i)
            w = jnp.concatenate([w_v[0, span, :], w_v[1, span, :]], axis=1)
            w_high, w_low = halves(w)
            total[:cols] += jnp.dot(
                split3(kept[:cols]),
                jnp.concatenate([w_high, w_low, w_high], axis=0),
                preferred_element_type=jnp.float32,
            )

        each_leaf(solve, couple)
        put(0, total[:half, :rank])
        put(1, total[half:cols, :rank])
        put(2, total[:half, rank:])
        put(3, total[half:cols, rank:])

    @pl.when((position == 1) | (position == 2))
    def _():
        mine = position - 1
        other = 2 - position
        total[...] = jnp.zeros_like(total)

        def solve(i, kept):
            span = span_of(i)
            x = jnp.concatenate([rhs_v[:, span], w_v[mine, span, :].T], axis=0)
            y = leaf_product(x, i)
            z[:, span] = y[:cols]
            lw[:rank, span] = y[cols:]
            kept[...] = y

        def couple(i, kept):
            w_high, w_low = halves(w_v[other, span_of(i), :])
            right = jnp.concatenate([w_high, w_low], axis=1)
            total[...] += jnp.dot(
                jnp.concatenate(halves(kept[...]), axis=1),
                jnp.concatenate([right, right], axis=0),
                preferred_element_type=jnp.float32,
            )

        each_leaf(solve, couple)
        summed = total[:, :rank] + total[:, rank:]

        @pl.when(position == 1)
        def _():
            put(0, summed[cols:])
            put(2, summed[:half])
            put(3, summed[half:cols])

        @pl.when(position == 2)
        def _():
            put(0, summed[:half])
            put(1, summed[half:cols])
            put(2, summed[cols:])

    @pl.when(position == 3)
    def _():
        def solve(i, kept):
            span = span_of(i)
            x = jnp.concatenate(
                [rhs_v[:, span], w_v[0, span, :].T, w_v[1, span, :].T], axis=0
            )
            y = leaf_product(x, i)
            z[:, span] = y[:cols]
            lw[:, span] = y[cols:]

        each_leaf(solve, lambda i, kept: None)


def main_call(rhs, linv, w_one, w_two, held):
    cols, rows = rhs.shape
    leaves, leaf, _ = linv.shape
    rank = w_one.shape[1]
    arrays = [
        pltpu.with_memory_space_constraint(v, pltpu.HBM)
        for v in (held, rhs, linv, w_one, w_two)
    ]
    return pl.pallas_call(
        main_kernel,
        in_specs=[pl.BlockSpec(memory_space=pltpu.HBM)] * 5,
        out_specs=[pl.BlockSpec(memory_space=pltpu.VMEM)] * 3,
        out_shape=[
            pltpu.VMEM((cols, rows), jnp.float32),
            pltpu.VMEM((2 * rank, rows), jnp.float32),
            pltpu.VMEM((2 * cols, rank), jnp.float32),
        ],
        scratch_shapes=[
            pltpu.SMEM(held.shape, jnp.int32),
            pltpu.VMEM((cols, rows), jnp.float32),
            pltpu.VMEM((leaves, leaf, leaf), jnp.float32),
            pltpu.VMEM((2, rows, rank), jnp.float32),
            pltpu.VMEM((cols + rank, 2 * rank), jnp.float32),
            pltpu.VMEM((cols + rank, leaf), jnp.float32),
            pltpu.VMEM((cols + rank, leaf), jnp.float32),
            pltpu.SemaphoreType.DMA(()),
            pltpu.SemaphoreType.DMA((4, leaves // GROUP)),
        ],
        compiler_params=pltpu.CompilerParams(vmem_limit_bytes=40 * 2**20),
        name="leaves",
    )(*arrays)


def pick_kernel(held, got, out, place, sums, trees):
    slots = held.shape[0]
    block = got.shape[0] // slots
    for s in range(slots):
        place[held[s]] = s
        value = got[s * block : s * block + TILE]
        for i in range(1, block // TILE):
            value = value + got[s * block + i * TILE : s * block + (i + 1) * TILE]
        value = value + pltpu.roll(value, TILE // 2, 0)
        sums[s * TILE : (s + 1) * TILE] = value
    row = lax.broadcasted_iota(jnp.int32, (TILE, got.shape[1]), 0)
    for t in range(slots // 4):

        def block_of(p):
            return sums[pl.ds(pl.multiple_of(place[4 * t + p] * TILE, TILE), TILE), :]

        a, b, c = block_of(0), block_of(1), block_of(2)
        tail = jnp.where(row == 6, pltpu.roll(b, 2, 0), pltpu.roll(c, 1, 0))
        tile = jnp.where(row < 2, a, jnp.where(row < 4, a + b, jnp.where(row < 6, c, tail)))
        trees[t * TILE : (t + 1) * TILE] = tile
    for s in range(slots):
        tile = trees[pl.ds(pl.multiple_of(held[s] // 4 * TILE, TILE), TILE), :]
        for i in range(PER_BLOCK):
            out[(s * PER_BLOCK + i) * TILE : (s * PER_BLOCK + i + 1) * TILE] = tile


def pick_call(got, held):
    rows, rank = got.shape
    slots = held.shape[0]
    return pl.pallas_call(
        pick_kernel,
        in_specs=[
            pl.BlockSpec(memory_space=pltpu.SMEM),
            pl.BlockSpec(memory_space=pltpu.VMEM),
        ],
        out_specs=pl.BlockSpec(memory_space=pltpu.VMEM),
        out_shape=pltpu.VMEM((slots * PER_BLOCK * TILE, rank), jnp.float32),
        scratch_shapes=[
            pltpu.SMEM((slots,), jnp.int32),
            pltpu.VMEM((slots * TILE, rank), jnp.float32),
            pltpu.VMEM((slots // 4 * TILE, rank), jnp.float32),
        ],
        compiler_params=pltpu.CompilerParams(vmem_limit_bytes=4 * 2**20),
        name="pick",
    )(held, pltpu.with_memory_space_constraint(got, pltpu.VMEM))


def last_kernel(scaling, held, ranks, got, z, lw, out, solved, sems):
    cols, rows = z.shape
    devices = got.shape[0] // TILE
    rank = got.shape[1]
    cluster = held[own_slot()]
    position = lax.rem(cluster, 4)
    tree = cluster // 4
    count = rows // CHUNK

    def mat(*rows):
        pieces = [got[pl.ds(j, devices, stride=TILE), :] for j in rows]
        return jnp.concatenate(pieces, axis=0)

    def masked(value, limit):
        lane = lax.broadcasted_iota(jnp.int32, value.shape, 1)
        return jnp.where(lane < limit, value * scaling, 0.0)

    def times(left, right):
        r_high, r_low = halves(right)
        return jnp.dot(
            left,
            jnp.concatenate([r_high, r_low, r_high], axis=0),
            preferred_element_type=jnp.float32,
        )

    def first():
        return masked(mat(0, 1), ranks[2 * tree])

    def second():
        value = mat(2, 3) - times(split3(first()), mat(6))
        return masked(value, ranks[8 + tree])

    def send(source, i):
        span = pl.ds(i * CHUNK, CHUNK)
        return pltpu.make_async_copy(source.at[:, span], out.at[:, span], sems.at[i])

    def correct(coef):
        depth = coef.shape[1]
        left = split3(coef)
        for i in range(count):
            span = slice(i * CHUNK, (i + 1) * CHUNK)
            solved[:, span] = z[:, span] - times(left, lw[:depth, span])
            send(solved, i).start()
        for i in range(count):
            send(solved, i).wait()

    @pl.when(position == 0)
    def _():
        for i in range(count):
            send(z, i).start()
        for i in range(count):
            send(z, i).wait()

    @pl.when(position == 1)
    def _():
        correct(first())

    @pl.when(position == 2)
    def _():
        correct(second())

    @pl.when(position == 3)
    def _():
        two = second()
        value = mat(4, 5) - times(split3(two), mat(7))
        correct(jnp.concatenate([masked(value, ranks[2 * tree + 1]), two], axis=1))


def last_call(got, z, lw, held, ranks, scaling):
    cols, rows = z.shape
    arrays = [pltpu.with_memory_space_constraint(v, pltpu.VMEM) for v in (got, z, lw)]
    return pl.pallas_call(
        functools.partial(last_kernel, scaling),
        in_specs=[pl.BlockSpec(memory_space=pltpu.SMEM)] * 2
        + [pl.BlockSpec(memory_space=pltpu.VMEM)] * 3,
        out_specs=pl.BlockSpec(memory_space=pltpu.HBM),
        out_shape=pltpu.HBM((cols, rows), jnp.float32),
        scratch_shapes=[
            pltpu.VMEM((cols, rows), jnp.float32),
            pltpu.SemaphoreType.DMA((rows // CHUNK,)),
        ],
        compiler_params=pltpu.CompilerParams(vmem_limit_bytes=16 * 2**20),
        name="correct",
    )(held, ranks, *arrays)


def swap(value):
    return lax.all_to_all(value, AXES, 0, 0, tiled=True)


def shards(rhs, linv, w_one, w_two, held, ranks):
    scaling = 1.0 / math.sqrt(rhs.shape[1] * PER_BLOCK)
    z, lw, msg = main_call(rhs, linv, w_one, w_two, held)
    shared = swap(pick_call(swap(msg), held))
    return last_call(shared, z, lw, held, ranks, scaling)


def solution(mesh):
    return jax.shard_map(
        shards,
        mesh=mesh,
        in_specs=(P(None, AXES), P(AXES, None, None), P(AXES, None), P(AXES, None), P(), P()),
        out_specs=P(None, AXES),
        check_vma=False,
    )
```

```python
import functools
import math

import jax
import jax.numpy as jnp
from jax import lax
from jax.experimental import pallas as pl
from jax.experimental.pallas import tpu as pltpu
from jax.sharding import PartitionSpec as P


AXES = ("clu", "row")
GROUP = 2
CHUNK = 512
PER_BLOCK = 8
TILE = 8


def halves(value):
    high = value.astype(jnp.bfloat16)
    low = (value - high.astype(jnp.float32)).astype(jnp.bfloat16)
    return high, low


def split3(value):
    high, low = halves(value)
    return jnp.concatenate([high, high, low], axis=1)


def nt(left, right):
    return lax.dot_general(
        left, right, (((1,), (1,)), ((), ())), preferred_element_type=jnp.float32
    )


def own_slot():
    device = lax.axis_index("clu") * lax.axis_size("row") + lax.axis_index("row")
    return device // PER_BLOCK


def main_kernel(
    held_in, rhs, linv, w_one, w_two, z, lw, msg,
    held, rhs_v, linv_v, w_v, total, kept_a, kept_b, held_sem, sems,
):
    cols = rhs.shape[0]
    leaves, leaf, _ = linv.shape
    rank = w_one.shape[1]
    groups = leaves // GROUP
    half = cols // 2

    def put(j, block):
        msg[pl.ds(j, half, stride=4), :] = block

    def copies(g):
        rows = pl.ds(g * (GROUP * leaf), GROUP * leaf)
        pair = pl.ds(g * GROUP, GROUP)
        return [
            pltpu.make_async_copy(rhs.at[:, rows], rhs_v.at[:, rows], sems.at[0, g]),
            pltpu.make_async_copy(linv.at[pair], linv_v.at[pair], sems.at[1, g]),
            pltpu.make_async_copy(w_one.at[rows], w_v.at[0, rows], sems.at[2, g]),
            pltpu.make_async_copy(w_two.at[rows], w_v.at[1, rows], sems.at[3, g]),
        ]

    held_copy = pltpu.make_async_copy(held_in, held, held_sem)
    held_copy.start()
    for g in range(groups):
        for copy in copies(g):
            copy.start()
    msg[...] = jnp.zeros_like(msg)
    held_copy.wait()
    position = lax.rem(held[own_slot()], 4)

    def span_of(i):
        return pl.ds(pl.multiple_of(i * leaf, leaf), leaf)

    def wait(g):
        for copy in copies(g):
            copy.wait()

    def each_pair(solve, couple):
        wait(0)
        solve(0, kept_a, 0)
        solve(1, kept_a, 1)

        def four(k, carry):
            wait(2 * k + 1)
            couple(4 * k, kept_a)
            solve(4 * k + 2, kept_b, 0)
            solve(4 * k + 3, kept_b, 1)
            wait(2 * k + 2)
            couple(4 * k + 2, kept_b)
            solve(4 * k + 4, kept_a, 0)
            solve(4 * k + 5, kept_a, 1)
            return carry

        lax.fori_loop(0, groups // 2 - 1, four, 0)
        wait(groups - 1)
        couple(leaves - 4, kept_a)
        solve(leaves - 2, kept_b, 0)
        solve(leaves - 1, kept_b, 1)
        couple(leaves - 2, kept_b)

    def each_leaf(solve, couple):
        even, odd = kept_a.at[0], kept_a.at[1]
        wait(0)
        solve(0, even)

        def pair(k, carry):
            wait(k + 1)
            solve(2 * k + 1, odd)
            couple(2 * k, even)
            solve(2 * k + 2, even)
            couple(2 * k + 1, odd)
            return carry

        lax.fori_loop(0, groups - 1, pair, 0)
        couple(leaves - 2, even)
        solve(leaves - 1, odd)
        couple(leaves - 1, odd)

    def leaf_product(x, i):
        l_high, l_low = halves(linv_v[i])
        return nt(split3(x), jnp.concatenate([l_high, l_low, l_high], axis=1))

    @pl.when(position == 0)
    def _():
        total[:cols] = jnp.zeros((cols, 2 * rank), jnp.float32)

        def solve(i, kept, j):
            span = span_of(i)
            y = leaf_product(rhs_v[:, span], i)
            z[:, span] = y
            kept[j, :cols] = y

        def couple(i, kept):
            left, right = [], []
            for j in range(2):
                span = span_of(i + j)
                w = jnp.concatenate([w_v[0, span, :], w_v[1, span, :]], axis=1)
                w_high, w_low = halves(w)
                left.append(split3(kept[j, :cols]))
                right += [w_high, w_low, w_high]
            total[:cols] += jnp.dot(
                jnp.concatenate(left, axis=1),
                jnp.concatenate(right, axis=0),
                preferred_element_type=jnp.float32,
            )

        each_pair(solve, couple)
        put(0, total[:half, :rank])
        put(1, total[half:cols, :rank])
        put(2, total[:half, rank:])
        put(3, total[half:cols, rank:])

    @pl.when((position == 1) | (position == 2))
    def _():
        mine = position - 1
        other = 2 - position
        total[...] = jnp.zeros_like(total)

        def solve(i, kept):
            span = span_of(i)
            x = jnp.concatenate([rhs_v[:, span], w_v[mine, span, :].T], axis=0)
            y = leaf_product(x, i)
            z[:, span] = y[:cols]
            lw[:rank, span] = y[cols:]
            kept[...] = y

        def couple(i, kept):
            w_high, w_low = halves(w_v[other, span_of(i), :])
            right = jnp.concatenate([w_high, w_low], axis=1)
            total[...] += jnp.dot(
                jnp.concatenate(halves(kept[...]), axis=1),
                jnp.concatenate([right, right], axis=0),
                preferred_element_type=jnp.float32,
            )

        each_leaf(solve, couple)
        summed = total[:, :rank] + total[:, rank:]

        @pl.when(position == 1)
        def _():
            put(0, summed[cols:])
            put(2, summed[:half])
            put(3, summed[half:cols])

        @pl.when(position == 2)
        def _():
            put(0, summed[:half])
            put(1, summed[half:cols])
            put(2, summed[cols:])

    @pl.when(position == 3)
    def _():
        def solve(i, kept, j):
            span = span_of(i)
            x = jnp.concatenate(
                [rhs_v[:, span], w_v[0, span, :].T, w_v[1, span, :].T], axis=0
            )
            y = leaf_product(x, i)
            z[:, span] = y[:cols]
            lw[:, span] = y[cols:]

        each_pair(solve, lambda i, kept: None)


def main_call(rhs, linv, w_one, w_two, held):
    cols, rows = rhs.shape
    leaves, leaf, _ = linv.shape
    rank = w_one.shape[1]
    arrays = [
        pltpu.with_memory_space_constraint(v, pltpu.HBM)
        for v in (held, rhs, linv, w_one, w_two)
    ]
    return pl.pallas_call(
        main_kernel,
        in_specs=[pl.BlockSpec(memory_space=pltpu.HBM)] * 5,
        out_specs=[pl.BlockSpec(memory_space=pltpu.VMEM)] * 3,
        out_shape=[
            pltpu.VMEM((cols, rows), jnp.float32),
            pltpu.VMEM((2 * rank, rows), jnp.float32),
            pltpu.VMEM((2 * cols, rank), jnp.float32),
        ],
        scratch_shapes=[
            pltpu.SMEM(held.shape, jnp.int32),
            pltpu.VMEM((cols, rows), jnp.float32),
            pltpu.VMEM((leaves, leaf, leaf), jnp.float32),
            pltpu.VMEM((2, rows, rank), jnp.float32),
            pltpu.VMEM((cols + rank, 2 * rank), jnp.float32),
            pltpu.VMEM((2, cols + rank, leaf), jnp.float32),
            pltpu.VMEM((2, cols + rank, leaf), jnp.float32),
            pltpu.SemaphoreType.DMA(()),
            pltpu.SemaphoreType.DMA((4, leaves // GROUP)),
        ],
        compiler_params=pltpu.CompilerParams(vmem_limit_bytes=40 * 2**20),
        name="leaves",
    )(*arrays)


def pick_kernel(held, got, out, place, sums, trees):
    slots = held.shape[0]
    block = got.shape[0] // slots
    for s in range(slots):
        place[held[s]] = s
        value = got[s * block : s * block + TILE]
        for i in range(1, block // TILE):
            value = value + got[s * block + i * TILE : s * block + (i + 1) * TILE]
        value = value + pltpu.roll(value, TILE // 2, 0)
        sums[s * TILE : (s + 1) * TILE] = value
    row = lax.broadcasted_iota(jnp.int32, (TILE, got.shape[1]), 0)
    for t in range(slots // 4):

        def block_of(p):
            return sums[pl.ds(pl.multiple_of(place[4 * t + p] * TILE, TILE), TILE), :]

        a, b, c = block_of(0), block_of(1), block_of(2)
        tail = jnp.where(row == 6, pltpu.roll(b, 2, 0), pltpu.roll(c, 1, 0))
        tile = jnp.where(row < 2, a, jnp.where(row < 4, a + b, jnp.where(row < 6, c, tail)))
        trees[t * TILE : (t + 1) * TILE] = tile
    for s in range(slots):
        tile = trees[pl.ds(pl.multiple_of(held[s] // 4 * TILE, TILE), TILE), :]
        for i in range(PER_BLOCK):
            out[(s * PER_BLOCK + i) * TILE : (s * PER_BLOCK + i + 1) * TILE] = tile


def pick_call(got, held):
    rows, rank = got.shape
    slots = held.shape[0]
    return pl.pallas_call(
        pick_kernel,
        in_specs=[
            pl.BlockSpec(memory_space=pltpu.SMEM),
            pl.BlockSpec(memory_space=pltpu.VMEM),
        ],
        out_specs=pl.BlockSpec(memory_space=pltpu.VMEM),
        out_shape=pltpu.VMEM((slots * PER_BLOCK * TILE, rank), jnp.float32),
        scratch_shapes=[
            pltpu.SMEM((slots,), jnp.int32),
            pltpu.VMEM((slots * TILE, rank), jnp.float32),
            pltpu.VMEM((slots // 4 * TILE, rank), jnp.float32),
        ],
        compiler_params=pltpu.CompilerParams(vmem_limit_bytes=4 * 2**20),
        name="pick",
    )(held, pltpu.with_memory_space_constraint(got, pltpu.VMEM))


def last_kernel(scaling, held, ranks, got, z, lw, out, solved, sems):
    cols, rows = z.shape
    devices = got.shape[0] // TILE
    rank = got.shape[1]
    cluster = held[own_slot()]
    position = lax.rem(cluster, 4)
    tree = cluster // 4
    count = rows // CHUNK

    def mat(*rows):
        pieces = [got[pl.ds(j, devices, stride=TILE), :] for j in rows]
        return jnp.concatenate(pieces, axis=0)

    def masked(value, limit):
        lane = lax.broadcasted_iota(jnp.int32, value.shape, 1)
        return jnp.where(lane < limit, value * scaling, 0.0)

    def times(left, right):
        r_high, r_low = halves(right)
        return jnp.dot(
            left,
            jnp.concatenate([r_high, r_low, r_high], axis=0),
            preferred_element_type=jnp.float32,
        )

    def first():
        return masked(mat(0, 1), ranks[2 * tree])

    def second():
        value = mat(2, 3) - times(split3(first()), mat(6))
        return masked(value, ranks[8 + tree])

    def send(source, i):
        span = pl.ds(i * CHUNK, CHUNK)
        return pltpu.make_async_copy(source.at[:, span], out.at[:, span], sems.at[i])

    def correct(coef):
        depth = coef.shape[1]
        left = split3(coef)
        for i in range(count):
            span = slice(i * CHUNK, (i + 1) * CHUNK)
            solved[:, span] = z[:, span] - times(left, lw[:depth, span])
            send(solved, i).start()
        for i in range(count):
            send(solved, i).wait()

    @pl.when(position == 0)
    def _():
        for i in range(count):
            send(z, i).start()
        for i in range(count):
            send(z, i).wait()

    @pl.when(position == 1)
    def _():
        correct(first())

    @pl.when(position == 2)
    def _():
        correct(second())

    @pl.when(position == 3)
    def _():
        two = second()
        value = mat(4, 5) - times(split3(two), mat(7))
        correct(jnp.concatenate([masked(value, ranks[2 * tree + 1]), two], axis=1))


def last_call(got, z, lw, held, ranks, scaling):
    cols, rows = z.shape
    arrays = [pltpu.with_memory_space_constraint(v, pltpu.VMEM) for v in (got, z, lw)]
    return pl.pallas_call(
        functools.partial(last_kernel, scaling),
        in_specs=[pl.BlockSpec(memory_space=pltpu.SMEM)] * 2
        + [pl.BlockSpec(memory_space=pltpu.VMEM)] * 3,
        out_specs=pl.BlockSpec(memory_space=pltpu.HBM),
        out_shape=pltpu.HBM((cols, rows), jnp.float32),
        scratch_shapes=[
            pltpu.VMEM((cols, rows), jnp.float32),
            pltpu.SemaphoreType.DMA((rows // CHUNK,)),
        ],
        compiler_params=pltpu.CompilerParams(vmem_limit_bytes=16 * 2**20),
        name="correct",
    )(held, ranks, *arrays)


def swap(value):
    return lax.all_to_all(value, AXES, 0, 0, tiled=True)


def shards(rhs, linv, w_one, w_two, held, ranks):
    scaling = 1.0 / math.sqrt(rhs.shape[1] * PER_BLOCK)
    z, lw, msg = main_call(rhs, linv, w_one, w_two, held)
    shared = swap(pick_call(swap(msg), held))
    return last_call(shared, z, lw, held, ranks, scaling)


def solution(mesh):
    return jax.shard_map(
        shards,
        mesh=mesh,
        in_specs=(P(None, AXES), P(AXES, None, None), P(AXES, None), P(AXES, None), P(), P()),
        out_specs=P(None, AXES),
        check_vma=False,
    )
```

```python
import functools
import math

import jax
import jax.numpy as jnp
from jax import lax
from jax.experimental import pallas as pl
from jax.experimental.pallas import tpu as pltpu
from jax.sharding import PartitionSpec as P


AXES = ("clu", "row")
GROUP = 2
CHUNK = 512
PER_BLOCK = 8
TILE = 8


def halves(value):
    high = value.astype(jnp.bfloat16)
    low = (value - high.astype(jnp.float32)).astype(jnp.bfloat16)
    return high, low


def split3(value):
    high, low = halves(value)
    return jnp.concatenate([high, high, low], axis=1)


def nt(left, right):
    return lax.dot_general(
        left, right, (((1,), (1,)), ((), ())), preferred_element_type=jnp.float32
    )


def own_slot():
    device = lax.axis_index("clu") * lax.axis_size("row") + lax.axis_index("row")
    return device // PER_BLOCK


def main_kernel(
    held_in, rhs, linv, w_one, w_two, z, lw, msg,
    held, rhs_v, linv_v, w_v, total, kept_a, kept_b, held_sem, sems,
):
    cols = rhs.shape[0]
    leaves, leaf, _ = linv.shape
    rank = w_one.shape[1]
    groups = leaves // GROUP
    half = cols // 2

    def put(j, block):
        msg[pl.ds(j, half, stride=4), :] = block

    def copies(g):
        rows = pl.ds(g * (GROUP * leaf), GROUP * leaf)
        pair = pl.ds(g * GROUP, GROUP)
        return [
            pltpu.make_async_copy(rhs.at[:, rows], rhs_v.at[:, rows], sems.at[0, g]),
            pltpu.make_async_copy(linv.at[pair], linv_v.at[pair], sems.at[1, g]),
            pltpu.make_async_copy(w_one.at[rows], w_v.at[0, rows], sems.at[2, g]),
            pltpu.make_async_copy(w_two.at[rows], w_v.at[1, rows], sems.at[3, g]),
        ]

    held_copy = pltpu.make_async_copy(held_in, held, held_sem)
    held_copy.start()
    for g in range(groups):
        for copy in copies(g):
            copy.start()
    msg[...] = jnp.zeros_like(msg)
    held_copy.wait()
    position = lax.rem(held[own_slot()], 4)

    def span_of(i):
        return pl.ds(pl.multiple_of(i * leaf, leaf), leaf)

    def wait(g):
        for copy in copies(g):
            copy.wait()

    def each_pair(solve, couple):
        wait(0)
        solve(0, kept_a, 0)
        solve(1, kept_a, 1)

        def four(k, carry):
            wait(2 * k + 1)
            couple(4 * k, kept_a)
            solve(4 * k + 2, kept_b, 0)
            solve(4 * k + 3, kept_b, 1)
            wait(2 * k + 2)
            couple(4 * k + 2, kept_b)
            solve(4 * k + 4, kept_a, 0)
            solve(4 * k + 5, kept_a, 1)
            return carry

        lax.fori_loop(0, groups // 2 - 1, four, 0)
        wait(groups - 1)
        couple(leaves - 4, kept_a)
        solve(leaves - 2, kept_b, 0)
        solve(leaves - 1, kept_b, 1)
        couple(leaves - 2, kept_b)

    def each_leaf(solve, couple):
        even, odd = kept_a.at[0], kept_a.at[1]
        wait(0)
        solve(0, even)

        def pair(k, carry):
            wait(k + 1)
            solve(2 * k + 1, odd)
            couple(2 * k, even)
            solve(2 * k + 2, even)
            couple(2 * k + 1, odd)
            return carry

        lax.fori_loop(0, groups - 1, pair, 0)
        couple(leaves - 2, even)
        solve(leaves - 1, odd)
        couple(leaves - 1, odd)

    def leaf_product(x, i):
        l_high, l_low = halves(linv_v[i])
        return nt(split3(x), jnp.concatenate([l_high, l_low, l_high], axis=1))

    @pl.when(position == 0)
    def _():
        total[:cols] = jnp.zeros((cols, 2 * rank), jnp.float32)

        def solve(i, kept, j):
            span = span_of(i)
            y = leaf_product(rhs_v[:, span], i)
            z[:, span] = y
            kept[j, :cols] = y

        def couple(i, kept):
            left, right = [], []
            for j in range(2):
                span = span_of(i + j)
                w = jnp.concatenate([w_v[0, span, :], w_v[1, span, :]], axis=1)
                w_high, w_low = halves(w)
                left.append(split3(kept[j, :cols]))
                right += [w_high, w_low, w_high]
            total[:cols] += jnp.dot(
                jnp.concatenate(left, axis=1),
                jnp.concatenate(right, axis=0),
                preferred_element_type=jnp.float32,
            )

        each_pair(solve, couple)
        put(0, total[:half, :rank])
        put(1, total[half:cols, :rank])
        put(2, total[:half, rank:])
        put(3, total[half:cols, rank:])

    def middle(mine, other):
        total[...] = jnp.zeros_like(total)

        def solve(i, kept):
            span = span_of(i)
            x = jnp.concatenate([rhs_v[:, span], w_v[mine, span, :].T], axis=0)
            y = leaf_product(x, i)
            z[:, span] = y[:cols]
            lw[:rank, span] = y[cols:]
            kept[...] = y

        def couple(i, kept):
            w_high, w_low = halves(w_v[other, span_of(i), :])
            right = jnp.concatenate([w_high, w_low], axis=1)
            total[...] += jnp.dot(
                jnp.concatenate(halves(kept[...]), axis=1),
                jnp.concatenate([right, right], axis=0),
                preferred_element_type=jnp.float32,
            )

        each_leaf(solve, couple)
        summed = total[:, :rank] + total[:, rank:]

        if mine == 0:
            put(0, summed[cols:])
            put(2, summed[:half])
            put(3, summed[half:cols])
        else:
            put(0, summed[:half])
            put(1, summed[half:cols])
            put(2, summed[cols:])

    pl.when(position == 1)(lambda: middle(0, 1))
    pl.when(position == 2)(lambda: middle(1, 0))

    @pl.when(position == 3)
    def _():
        def solve(i, kept, j):
            span = span_of(i)
            x = jnp.concatenate(
                [rhs_v[:, span], w_v[0, span, :].T, w_v[1, span, :].T], axis=0
            )
            y = leaf_product(x, i)
            z[:, span] = y[:cols]
            lw[:, span] = y[cols:]

        each_pair(solve, lambda i, kept: None)


def main_call(rhs, linv, w_one, w_two, held):
    cols, rows = rhs.shape
    leaves, leaf, _ = linv.shape
    rank = w_one.shape[1]
    arrays = [
        pltpu.with_memory_space_constraint(v, pltpu.HBM)
        for v in (held, rhs, linv, w_one, w_two)
    ]
    return pl.pallas_call(
        main_kernel,
        in_specs=[pl.BlockSpec(memory_space=pltpu.HBM)] * 5,
        out_specs=[pl.BlockSpec(memory_space=pltpu.VMEM)] * 3,
        out_shape=[
            pltpu.VMEM((cols, rows), jnp.float32),
            pltpu.VMEM((2 * rank, rows), jnp.float32),
            pltpu.VMEM((2 * cols, rank), jnp.float32),
        ],
        scratch_shapes=[
            pltpu.SMEM(held.shape, jnp.int32),
            pltpu.VMEM((cols, rows), jnp.float32),
            pltpu.VMEM((leaves, leaf, leaf), jnp.float32),
            pltpu.VMEM((2, rows, rank), jnp.float32),
            pltpu.VMEM((cols + rank, 2 * rank), jnp.float32),
            pltpu.VMEM((2, cols + rank, leaf), jnp.float32),
            pltpu.VMEM((2, cols + rank, leaf), jnp.float32),
            pltpu.SemaphoreType.DMA(()),
            pltpu.SemaphoreType.DMA((4, leaves // GROUP)),
        ],
        compiler_params=pltpu.CompilerParams(vmem_limit_bytes=40 * 2**20),
        name="leaves",
    )(*arrays)


def pick_kernel(held, got, out, place, sums, trees):
    slots = held.shape[0]
    block = got.shape[0] // slots
    for s in range(slots):
        place[held[s]] = s
        value = got[s * block : s * block + TILE]
        for i in range(1, block // TILE):
            value = value + got[s * block + i * TILE : s * block + (i + 1) * TILE]
        value = value + pltpu.roll(value, TILE // 2, 0)
        sums[s * TILE : (s + 1) * TILE] = value
    row = lax.broadcasted_iota(jnp.int32, (TILE, got.shape[1]), 0)
    for t in range(slots // 4):

        def block_of(p):
            return sums[pl.ds(pl.multiple_of(place[4 * t + p] * TILE, TILE), TILE), :]

        a, b, c = block_of(0), block_of(1), block_of(2)
        tail = jnp.where(row == 6, pltpu.roll(b, 2, 0), pltpu.roll(c, 1, 0))
        tile = jnp.where(row < 2, a, jnp.where(row < 4, a + b, jnp.where(row < 6, c, tail)))
        trees[t * TILE : (t + 1) * TILE] = tile
    for s in range(slots):
        tile = trees[pl.ds(pl.multiple_of(held[s] // 4 * TILE, TILE), TILE), :]
        for i in range(PER_BLOCK):
            out[(s * PER_BLOCK + i) * TILE : (s * PER_BLOCK + i + 1) * TILE] = tile


def pick_call(got, held):
    rows, rank = got.shape
    slots = held.shape[0]
    return pl.pallas_call(
        pick_kernel,
        in_specs=[
            pl.BlockSpec(memory_space=pltpu.SMEM),
            pl.BlockSpec(memory_space=pltpu.VMEM),
        ],
        out_specs=pl.BlockSpec(memory_space=pltpu.VMEM),
        out_shape=pltpu.VMEM((slots * PER_BLOCK * TILE, rank), jnp.float32),
        scratch_shapes=[
            pltpu.SMEM((slots,), jnp.int32),
            pltpu.VMEM((slots * TILE, rank), jnp.float32),
            pltpu.VMEM((slots // 4 * TILE, rank), jnp.float32),
        ],
        compiler_params=pltpu.CompilerParams(vmem_limit_bytes=4 * 2**20),
        name="pick",
    )(held, pltpu.with_memory_space_constraint(got, pltpu.VMEM))


def last_kernel(scaling, held, ranks, got, z, lw, out, solved, sems):
    cols, rows = z.shape
    devices = got.shape[0] // TILE
    rank = got.shape[1]
    cluster = held[own_slot()]
    position = lax.rem(cluster, 4)
    tree = cluster // 4
    count = rows // CHUNK

    def mat(*rows):
        pieces = [got[pl.ds(j, devices, stride=TILE), :] for j in rows]
        return jnp.concatenate(pieces, axis=0)

    def masked(value, limit):
        lane = lax.broadcasted_iota(jnp.int32, value.shape, 1)
        return jnp.where(lane < limit, value * scaling, 0.0)

    def times(left, right):
        r_high, r_low = halves(right)
        return jnp.dot(
            left,
            jnp.concatenate([r_high, r_low, r_high], axis=0),
            preferred_element_type=jnp.float32,
        )

    def first():
        return masked(mat(0, 1), ranks[2 * tree])

    def second():
        value = mat(2, 3) - times(split3(first()), mat(6))
        return masked(value, ranks[8 + tree])

    def send(source, i):
        span = pl.ds(i * CHUNK, CHUNK)
        return pltpu.make_async_copy(source.at[:, span], out.at[:, span], sems.at[i])

    def correct(coef):
        depth = coef.shape[1]
        left = split3(coef)
        for i in range(count):
            span = slice(i * CHUNK, (i + 1) * CHUNK)
            solved[:, span] = z[:, span] - times(left, lw[:depth, span])
            send(solved, i).start()
        for i in range(count):
            send(solved, i).wait()

    @pl.when(position == 0)
    def _():
        for i in range(count):
            send(z, i).start()
        for i in range(count):
            send(z, i).wait()

    @pl.when(position == 1)
    def _():
        correct(first())

    @pl.when(position == 2)
    def _():
        correct(second())

    @pl.when(position == 3)
    def _():
        two = second()
        value = mat(4, 5) - times(split3(two), mat(7))
        correct(jnp.concatenate([masked(value, ranks[2 * tree + 1]), two], axis=1))


def last_call(got, z, lw, held, ranks, scaling):
    cols, rows = z.shape
    arrays = [pltpu.with_memory_space_constraint(v, pltpu.VMEM) for v in (got, z, lw)]
    return pl.pallas_call(
        functools.partial(last_kernel, scaling),
        in_specs=[pl.BlockSpec(memory_space=pltpu.SMEM)] * 2
        + [pl.BlockSpec(memory_space=pltpu.VMEM)] * 3,
        out_specs=pl.BlockSpec(memory_space=pltpu.HBM),
        out_shape=pltpu.HBM((cols, rows), jnp.float32),
        scratch_shapes=[
            pltpu.VMEM((cols, rows), jnp.float32),
            pltpu.SemaphoreType.DMA((rows // CHUNK,)),
        ],
        compiler_params=pltpu.CompilerParams(vmem_limit_bytes=16 * 2**20),
        name="correct",
    )(held, ranks, *arrays)


def swap(value):
    return lax.all_to_all(value, AXES, 0, 0, tiled=True)


def shards(rhs, linv, w_one, w_two, held, ranks):
    scaling = 1.0 / math.sqrt(rhs.shape[1] * PER_BLOCK)
    z, lw, msg = main_call(rhs, linv, w_one, w_two, held)
    shared = swap(pick_call(swap(msg), held))
    return last_call(shared, z, lw, held, ranks, scaling)


def solution(mesh):
    return jax.shard_map(
        shards,
        mesh=mesh,
        in_specs=(P(None, AXES), P(AXES, None, None), P(AXES, None), P(AXES, None), P(), P()),
        out_specs=P(None, AXES),
        check_vma=False,
    )
```
